256 devices in a mesh: row: 16 (over x_hi, y, core), col: 16 (over x_lo, z).
Axes of the slice: x: 4 (x_hi: 2, x_lo: 2; x = x_hi * 2 + x_lo), y: 4, z: 8, core: 2. Of those that a mesh axis runs over, the one named last changes fastest.
Arguments:
- test_block: bfloat16 [512, 32768], P('col', 'row'), may hold values from -6 to 6
- inverse_gram: bfloat16 [32768, 32768], P('row', 'col'), may hold values from -0.03125 to 0.03125
- train_grads: bfloat16 [8192, 32768], P('col', 'row'), may hold values from -0.03125 to 0.03125
Outputs:
- scores: float32 [512, 8192], P('row', 'col')
The draws below stay inside these ranges and needn't reach their ends.
All inputs are finite; a program needn't handle non-finite values.
Results may differ from the reference program's by a relative error of at most 0.0029.
Values may be sent and summed in bfloat16 or wider, within the bound.
A program may use at most 64 MiB of HBM per device.

```python
import jax
import jax.numpy as jnp

NQ = 512
FEATS = 32768
DOCS = 8192


def level_of(own_key, shape, split, low, top_value):
    gain, own = 1.0, jax.random.fold_in(own_key, 6)
    for position, shards_of in split:
        draws = jnp.exp(jax.random.uniform(jax.random.fold_in(own, position), (shards_of,), jnp.float32, low / len(split), top_value / len(split)))
        gain = gain * jnp.repeat(draws, shape[position] // shards_of).reshape([-1 if axis == position else 1 for axis in range(len(shape))])
    return gain


def normal_values(stream_key, extent, spread, bound, split=(), kind=jnp.bfloat16):
    result = jax.random.normal(stream_key, extent, jnp.float32) * spread
    if len(split) > 0:
        result = level_of(stream_key, extent, split, -0.22, 0.18) * result
    return jnp.clip(result, min=-bound, max=bound).astype(kind)


def setup_inputs(seed: int = 0) -> dict:
    splits = jax.random.split(jax.random.key(seed), 4)
    return {
        "test_block": normal_values(splits[0], (NQ, FEATS), 1.0, 6.0, ((0, 16), (1, 16))),
        "inverse_gram": normal_values(splits[1], (FEATS, FEATS), FEATS ** -0.5, 0.03125, ((0, 16), (1, 16))),
        "train_grads": normal_values(splits[2], (DOCS, FEATS), FEATS ** -0.5, 0.03125, ((0, 16), (1, 16))),
    }


def reference(test_block, inverse_gram, train_grads):
    conditioned = jnp.dot(test_block, inverse_gram, preferred_element_type=jnp.float32).astype(jnp.bfloat16)
    return jnp.dot(conditioned, train_grads.T, preferred_element_type=jnp.float32)
```

```python
import jax
import jax.numpy as jnp
from jax import lax
from jax.experimental import pallas as pl
from jax.experimental.pallas import tpu as pltpu
from jax.sharding import PartitionSpec as P

MESH = pl.DeviceIdType.MESH
A, C = 0, 1
CUT_A, CUT_C = 896, 112


def kernel(
    t_hbm, g_hbm, d_hbm, out_ref,
    tb, gb, db, part, xr, bs, br, ms, cb, s, dx, ds_, dr,
    load_sem, ag_send, ag_recv, x_send, x_recv, b_send, b_recv,
    m_send, m_recv, e_send, e_recv, d_send, d_recv,
):
    row, col = lax.axis_index("row"), lax.axis_index("col")
    j, k = row // 2, row % 2
    xl, z = col // 8, col % 8
    other = 1 - k

    def zdev(dz):
        return (row, xl * 8 + (z + dz) % 8)

    xdev = (row, (1 - xl) * 8 + z)
    coredev = (j * 2 + other, col)

    def plane(jj):
        return (jj * 2 + k, col)

    move_to = (col, (1 - k) * 8 + j)
    move_from = (2 * z + 1 - xl, row)

    loads = {}

    def load(name, src, dst, sem):
        c = pltpu.make_async_copy(src, dst, load_sem.at[sem])
        c.start()
        loads[name] = c

    def jt(t):
        return (j + 1 + t) % 8

    def slot(ph, mx, dz):
        zz, xx = (z + dz) % 8, jnp.where(mx, 1 - xl, xl)
        if ph == A:
            return (zz % 2) * 8 + xx * 4 + zz // 2
        return zz * 2 + 1 - xx

    load("t0", t_hbm.at[pl.ds(0, 16)], tb.at[0, pl.ds(pl.multiple_of(slot(A, False, 0) * 16, 16), 16)], 0)
    load("t1", t_hbm.at[pl.ds(16, 16)], tb.at[1, pl.ds(pl.multiple_of(slot(A, False, 0) * 16, 16), 16)], 1)
    for t in range(8):
        load(("g", t), g_hbm.at[:, pl.ds(pl.multiple_of(jt(t) * 256, 256), 256)], gb.at[jt(t)], 2 + t)
    for t in range(8):
        load(("d", t), d_hbm.at[:, pl.ds(t * 256, 256)], db.at[t], 10 + t)

    barrier = pltpu.get_barrier_semaphore()
    for to in [zdev(1), zdev(-1), xdev, coredev, move_from] + [plane((j + i) % 8) for i in range(1, 8)]:
        pl.semaphore_signal(barrier, inc=1, device_id=to, device_id_type=MESH)
    pl.semaphore_wait(barrier, 12)

    sent = []

    def remote(src, dst, ssem, rsem, to):
        return pltpu.make_async_remote_copy(
            src_ref=src, dst_ref=dst, send_sem=ssem, recv_sem=rsem, device_id=to, device_id_type=MESH
        )

    def start(c):
        c.start()
        sent.append(c)

    def block(ph, h, mx, dz, piece):
        sl = slot(ph, mx, dz)
        if ph == A:
            r = pl.ds(pl.multiple_of(sl * 16, 16), 16)
            if piece == "w":
                return tb.at[h, r]
            if piece == "xf":
                return tb.at[h, r, pl.ds(0, CUT_A)]
            return tb.at[h, r, pl.ds(CUT_A, 2048 - CUT_A)]
        if piece == "w":
            return cb.at[h, sl]
        if piece == "xf":
            return cb.at[h, sl, pl.ds(0, CUT_C)]
        return cb.at[h, sl, pl.ds(CUT_C, 256 - CUT_C)]

    def message(ph, h, kind, dr_, d):
        i = 2 * ph + h
        if kind == "X":
            dz, n = d, 16 + d % 8
            piece = "w" if d == 0 else "zf"
            return ((ph, h, False, dz, piece), (ph, h, True, dz, piece), i, n, xdev)
        sign = 1 if dr_ == 0 else -1
        mx, piece, n = (False, "w", 0) if kind == "W" else (True, "xf", 8)
        src = (ph, h, mx, -sign * (d - 1), piece)
        dst = (ph, h, mx, -sign * d, piece)
        return (src, dst, i, n + dr_ * 4 + d - 1, zdev(sign))

    def send(ph, h, kind, dr_, d):
        src, _, i, n, to = message(ph, h, kind, dr_, d)
        ref = block(*src)
        source = ref
        if ph == A and src[2] is False and src[3] == 0:
            source = t_hbm.at[pl.ds(16 * h, 16)]
        start(remote(source, ref, ag_send.at[i, n], ag_recv.at[i, n], to))

    def arrived(ph, h, kind, dr_, d):
        _, dst, i, n, to = message(ph, h, kind, dr_, d)
        ref = block(*dst)
        remote(ref, ref, ag_send.at[i, n], ag_recv.at[i, n], to).wait_recv()

    def exists(h, kind, dr_, d):
        return d <= 3 or (d == 4 and (dr_ == h) == (kind == "W"))

    def ag_start(ph, h):
        send(ph, h, "X", 0, 0)
        send(ph, h, "W", 0, 1)
        send(ph, h, "W", 1, 1)

    def ag_step(ph, h, d):
        if d == 0:
            arrived(ph, h, "X", 0, 0)
            for dr_ in (0, 1):
                send(ph, h, "P", dr_, 1)
            return
        for kind in ("W", "P"):
            for dr_ in (0, 1):
                if not exists(h, kind, dr_, d):
                    continue
                arrived(ph, h, kind, dr_, d)
                if exists(h, kind, dr_, d + 1):
                    send(ph, h, kind, dr_, d + 1)
                if kind == "W":
                    send(ph, h, "X", 0, -d if dr_ == 0 else d)

    def ag_x(ph, h, d):
        for dz in ((0,) if d == 0 else (-d, d) if d < 4 else (4 if h == 1 else -4,)):
            if dz != 0:
                arrived(ph, h, "X", 0, dz)

    def mm(h, t):
        if h == 0:
            loads[("g", t)].wait()
        jj = jt(t)
        p = jnp.dot(tb[h], gb[jj], preferred_element_type=jnp.float32)
        part[h, jj, 0] = p[:, :128]
        part[h, jj, 1] = p[:, 128:]
        start(remote(part.at[h, jj, other], xr.at[h, jj], x_send.at[h, t], x_recv.at[h, t], coredev))

    def ex(h, t):
        jj = jt(t)
        remote(part.at[h, jj, other], xr.at[h, jj], x_send.at[h, t], x_recv.at[h, t], coredev).wait_recv()
        if t < 7:
            bs[h, jj] = (part[h, jj, k] + xr[h, jj]).astype(jnp.bfloat16)
            start(remote(bs.at[h, jj], br.at[h, j], b_send.at[h, t], b_recv.at[h, t], plane(jj)))

    def b_red(h):
        acc = part[h, j, k] + xr[h, j]
        for t in range(7):
            jj = (j + 7 - t) % 8
            remote(bs.at[h, 0], br.at[h, jj], b_send.at[h, t], b_recv.at[h, t], plane(jj)).wait_recv()
            acc = acc + br[h, jj].astype(jnp.float32)
        ms[h] = acc.astype(jnp.bfloat16)
        start(remote(ms.at[h], cb.at[h, 2 * j + k], m_send.at[h], m_recv.at[h], move_to))

    def c_start(h):
        own = cb.at[h, slot(C, False, 0)]
        remote(ms.at[h], own, m_send.at[h], m_recv.at[h], move_to).wait_recv()
        ag_start(C, h)

    def mm2(h, d):
        ag_x(C, h, d)
        for dz in (0,) if d == 0 else (-d, d) if d < 4 else (4,):
            zz = (z + dz) % 8
            lhs = jnp.concatenate([cb[h, 2 * zz], cb[h, 2 * zz + 1]], axis=1)
            v = lax.dot_general(lhs, db[zz], (((1,), (1,)), ((), ())), preferred_element_type=jnp.float32)
            if d == 0:
                s[h] = v
            else:
                s[h] += v

    def half(q):
        return pl.ds(pl.multiple_of(q * 128, 128), 128)

    def d_copy(h):
        return remote(s.at[h, half(other)], dx.at[h], e_send.at[h], e_recv.at[h], coredev)

    def d_start(h):
        start(d_copy(h))

    def d_send_(h):
        d_copy(h).wait_recv()
        ds_[h] = s[h, half(k)] + dx[h]
        for t in range(7):
            jj = jt(t)
            start(remote(ds_.at[h, pl.ds(pl.multiple_of(jj * 16, 16), 16)], dr.at[h, j], d_send.at[h, t], d_recv.at[h, t], plane(jj)))

    def d_red(h):
        acc = ds_[h, pl.ds(pl.multiple_of(j * 16, 16), 16)]
        for t in range(7):
            jj = (j + 7 - t) % 8
            remote(dr.at[h, jj], dr.at[h, jj], d_send.at[h, t], d_recv.at[h, t], plane(jj)).wait_recv()
            acc = acc + dr[h, jj]
        out_ref[pl.ds(16 * h, 16)] = acc

    ag_start(A, 0)
    ag_step(A, 0, 0)
    ag_start(A, 1)
    ag_step(A, 0, 1)
    ag_step(A, 1, 0)
    ag_step(A, 0, 2)
    ag_step(A, 1, 1)
    ag_step(A, 0, 3)
    ag_step(A, 1, 2)
    ag_step(A, 0, 4)
    for d in range(1, 5):
        ag_x(A, 0, d)
    loads["t0"].wait()
    for t in range(8):
        mm(0, t)
        if t >= 2:
            ex(0, t - 2)
        if t == 3:
            ag_step(A, 1, 3)
        if t == 7:
            ag_step(A, 1, 4)
    for t in (6, 7):
        ex(0, t)
    for d in range(1, 5):
        ag_x(A, 1, d)
    loads["t1"].wait()
    for t in range(8):
        mm(1, t)
        if t >= 2:
            ex(1, t - 2)
    for t in (6, 7):
        ex(1, t)
    for t in range(8):
        loads[("d", t)].wait()
    b_red(0)
    c_start(0)
    ag_step(C, 0, 0)
    ag_step(C, 0, 1)
    b_red(1)
    mm2(0, 0)
    ag_step(C, 0, 2)
    c_start(1)
    mm2(0, 1)
    ag_step(C, 0, 3)
    ag_step(C, 1, 0)
    mm2(0, 2)
    ag_step(C, 0, 4)
    ag_step(C, 1, 1)
    mm2(0, 3)
    mm2(1, 0)
    mm2(0, 4)
    d_start(0)
    ag_step(C, 1, 2)
    mm2(1, 1)
    d_send_(0)
    ag_step(C, 1, 3)
    mm2(1, 2)
    ag_step(C, 1, 4)
    mm2(1, 3)
    mm2(1, 4)
    d_start(1)
    d_red(0)
    d_send_(1)
    d_red(1)
    for c in sent:
        c.wait_send()


def body(test_block, inverse_gram, train_grads):
    bf, f32 = jnp.bfloat16, jnp.float32
    dma = pltpu.SemaphoreType.DMA
    return pl.pallas_call(
        kernel,
        out_shape=jax.ShapeDtypeStruct((32, 512), f32),
        in_specs=[pl.BlockSpec(memory_space=pl.ANY)] * 3,
        out_specs=pl.BlockSpec(memory_space=pltpu.VMEM),
        scratch_shapes=[
            pltpu.VMEM((2, 256, 2048), bf),
            pltpu.VMEM((8, 2048, 256), bf),
            pltpu.VMEM((8, 512, 256), bf),
            pltpu.VMEM((2, 8, 2, 256, 128), f32),
            pltpu.VMEM((2, 8, 256, 128), f32),
            pltpu.VMEM((2, 8, 256, 128), bf),
            pltpu.VMEM((2, 8, 256, 128), bf),
            pltpu.VMEM((2, 256, 128), bf),
            pltpu.VMEM((2, 16, 256, 128), bf),
            pltpu.VMEM((2, 256, 512), f32),
            pltpu.VMEM((2, 128, 512), f32),
            pltpu.VMEM((2, 128, 512), f32),
            pltpu.VMEM((2, 8, 16, 512), f32),
            dma((18,)),
            dma((4, 24)), dma((4, 24)),
            dma((2, 8)), dma((2, 8)),
            dma((2, 8)), dma((2, 8)),
            dma((2,)), dma((2,)),
            dma((2,)), dma((2,)),
            dma((2, 8)), dma((2, 8)),
        ],
        compiler_params=pltpu.CompilerParams(
            collective_id=0, has_side_effects=True, vmem_limit_bytes=52 * 2**20
        ),
        cost_estimate=pl.CostEstimate(flops=5_400_000_000, bytes_accessed=11_000_000, transcendentals=0),
        name="scores_kernel",
    )(test_block, inverse_gram, train_grads)


def solution(mesh):
    return jax.shard_map(
        body,
        mesh=mesh,
        in_specs=(P("col", "row"), P("row", "col"), P("col", "row")),
        out_specs=P("row", "col"),
        check_vma=False,
    )
```

```python
import jax
import jax.numpy as jnp
from jax import lax
from jax.experimental import pallas as pl
from jax.experimental.pallas import tpu as pltpu
from jax.sharding import PartitionSpec as P

MESH = pl.DeviceIdType.MESH
A, C = 0, 1
CUT_A, CUT_C = 896, 112
NT = (((1,), (1,)), ((), ()))


def kernel(
    t_hbm, g_hbm, d_hbm, out_ref,
    tb, gb, db, own, bs, br, ms, cb, s, dx, ds_, dr,
    load_sem, ag_send, ag_recv, g_send, g_recv, f_send, f_recv, b_send, b_recv,
    m_send, m_recv, e_send, e_recv, d_send, d_recv,
):
    row, col = lax.axis_index("row"), lax.axis_index("col")
    j, k = row // 2, row % 2
    xh, y = j // 4, j % 4
    xl, z = col // 8, col % 8
    other = 1 - k
    sigma = 2 * y + xh
    u_own = (sigma + 4 * k) % 8

    def chip(sg):
        return (sg % 2) * 4 + sg // 2

    def zdev(dz):
        return (row, xl * 8 + (z + dz) % 8)

    def xzdev(dz):
        return (row, (1 - xl) * 8 + (z + dz) % 8)

    xdev = xzdev(0)
    coredev = (j * 2 + other, col)

    def plane(jj):
        return (jj * 2 + k, col)

    def turn(h, u):
        return u if h == 0 else (8 - u) % 8

    def move_to(h):
        return (col, ((1 - k + z) % 2) * 8 + (z + turn(h, u_own)) % 8)

    z_src = 2 * y + k

    def move_from(h):
        u = turn(h, (z - z_src) % 8)
        ks = (1 + xl + k) % 2
        return (chip((u + 4 * ks) % 8) * 2 + ks, xh * 8 + z_src)

    loads = {}

    def load(name, src, dst, sem):
        c = pltpu.make_async_copy(src, dst, load_sem.at[sem])
        c.start()
        loads[name] = c

    def tslot(h, c, mx, dz):
        zz, xx = (z + dz) % 8, jnp.where(mx, 1 - xl, xl)
        return tb.at[h, c, zz % 2, xx, zz // 2]

    def cslot(h, mx, dz):
        zz, xx = (z + dz) % 8, jnp.where(mx, 1 - xl, xl)
        return 2 * turn(h, (zz - z_src) % 8) + (1 + xx + k) % 2

    def tile(n):
        return (u_own // 2 + 1 + n) % 4

    for h in (0, 1):
        load(("t", h), t_hbm.at[pl.ds(16 * h, 16)], tslot(h, k, False, 0), h)
    for n in range(4):
        c0 = pl.multiple_of(k * 1024 + tile(n) * 256, 256)
        load(("g", n), g_hbm.at[:, pl.ds(c0, 256)], gb.at[k, tile(n)], 2 + n)
    for q in range(8):
        for kk in range(2):
            load(("d", q, kk), d_hbm.at[:, pl.ds(kk * 1024 + q * 128, 128)], db.at[q, :, pl.ds(kk * 128, 128)], 6 + 2 * q + kk)

    barrier = pltpu.get_barrier_semaphore()
    greet = [zdev(1), zdev(-1), xzdev(1), xzdev(-1), xdev, coredev, move_from(0), move_from(1)]
    for to in greet + [plane((j + i) % 8) for i in range(1, 8)]:
        pl.semaphore_signal(barrier, inc=1, device_id=to, device_id_type=MESH)
    pl.semaphore_wait(barrier, 15)

    sent = []

    def remote(src, dst, ssem, rsem, to):
        return pltpu.make_async_remote_copy(
            src_ref=src, dst_ref=dst, send_sem=ssem, recv_sem=rsem, device_id=to, device_id_type=MESH
        )

    def start(c):
        c.start()
        sent.append(c)

    def block(ph, h, mx, dz, piece, origin=False):
        if ph == A:
            cut = pl.ds(0, CUT_A) if piece == "x" else pl.ds(CUT_A, 2048 - CUT_A)
            if origin and not mx and dz == 0:
                return t_hbm.at[pl.ds(16 * h, 16), cut]
            return tslot(h, k, mx, dz).at[:, cut]
        cut = pl.ds(0, CUT_C) if piece == "x" else pl.ds(CUT_C, 256 - CUT_C)
        return cb.at[h, cslot(h, mx, dz), cut]

    def message(ph, h, kind, way, d):
        i = 2 * ph + h
        if kind in "XY":
            piece, n = ("z", 24 + d % 8) if kind == "X" else ("x", 32)
            return (ph, h, False, d, piece), (ph, h, True, d, piece), i, n, xdev
        sign = 1 if way == 0 else -1
        if kind == "E":
            return (ph, h, False, -sign * 3, "z"), (ph, h, True, -sign * 4, "z"), i, 28, xzdev(sign)
        mx, piece = kind == "p", "z" if kind == "z" else "x"
        n = "zxp".index(kind) * 8 + way * 4 + d - 1
        if kind == "p" and d == 1:
            return (ph, h, False, 0, piece), (ph, h, True, -sign, piece), i, n, xzdev(sign)
        return (ph, h, mx, -sign * (d - 1), piece), (ph, h, mx, -sign * d, piece), i, n, zdev(sign)

    def send(ph, h, kind, way, d):
        src, _, i, n, to = message(ph, h, kind, way, d)
        start(remote(block(*src, origin=True), block(*src), ag_send.at[i, n], ag_recv.at[i, n], to))

    def arrived(ph, h, kind, way, d):
        _, dst, i, n, to = message(ph, h, kind, way, d)
        ref = block(*dst)
        remote(ref, ref, ag_send.at[i, n], ag_recv.at[i, n], to).wait_recv()

    def exists(h, kind, way, d):
        return d <= 3 or (d == 4 and (way == h) == (kind != "p"))

    def ag_start(ph, h):
        for kind in "pzx":
            for way in (0, 1):
                send(ph, h, kind, way, 1)
        send(ph, h, "Y", 0, 0)
        send(ph, h, "X", 0, 0)

    def ag(ph, h, kind, d):
        for way in (0, 1):
            if exists(h, kind, way, d):
                arrived(ph, h, kind, way, d)
                if exists(h, kind, way, d + 1):
                    send(ph, h, kind, way, d + 1)
                if kind == "z" and d == 3 and way == h:
                    send(ph, h, "E", way, 4)
                if kind == "z" and d < 4:
                    send(ph, h, "X", 0, -d if way == 0 else d)

    def step(ph, h, d):
        for kind in "zpx":
            ag(ph, h, kind, d)

    def around(d):
        return (0,) if d == 0 else (-d, d) if d < 4 else (4,)

    def ag_x(ph, h, d):
        for dz in around(d):
            arrived(ph, h, "X", 0, dz)
        if d == 0:
            arrived(ph, h, "Y", 0, 0)

    def f_copy(h, dz):
        zz = (z + dz) % 8
        ref = tb.at[h, k, zz % 2, :, zz // 2]
        return remote(ref, ref, f_send.at[h, dz % 8], f_recv.at[h, dz % 8], coredev)

    def forward(h, d):
        ag_x(A, h, d)
        if d == 0:
            loads[("t", h)].wait()
        for dz in around(d):
            start(f_copy(h, dz))

    def forwarded(h):
        for dz in range(8):
            zz = (z + dz) % 8
            ref = tb.at[h, other, zz % 2, :, zz // 2]
            remote(ref, ref, f_send.at[h, dz], f_recv.at[h, dz], coredev).wait_recv()

    def g_copy(n):
        c0 = pl.multiple_of(other * 1024 + n * 256, 256)
        return remote(g_hbm.at[:, pl.ds(c0, 256)], gb.at[k, n], g_send.at[n], g_recv.at[n], coredev)

    def g_start():
        for n in range(4):
            start(g_copy(n))

    def g_wait():
        for n in range(4):
            loads[("g", n)].wait()
            remote(gb.at[other, n], gb.at[other, n], g_send.at[n], g_recv.at[n], coredev).wait_recv()

    def mm(h, n):
        nn = tile(n)
        p = jnp.dot(tb[h, 0].reshape(256, 2048), gb[0, nn], preferred_element_type=jnp.float32)
        p = p + jnp.dot(tb[h, 1].reshape(256, 2048), gb[1, nn], preferred_element_type=jnp.float32)
        for e in (0, 1):
            u = 2 * nn + e
            pe = p[:, e * 128 : e * 128 + 128]

            def away():
                bs[h, u] = pe.astype(jnp.bfloat16)
                b_copy(h, u).start()

            if n < 3:
                away()
            else:
                pl.when(u != u_own)(away)

                @pl.when(u == u_own)
                def _():
                    own[h] = pe

    def b_copy(h, u):
        sg = (u - 4 * k) % 8
        n = (sg - sigma) % 8
        return remote(bs.at[h, u], br.at[h, n], b_send.at[h, n], b_recv.at[h, n], plane(chip(sg)))

    def b_red(h):
        acc = own[h]
        for n in range(1, 8):
            remote(bs.at[h, 0], br.at[h, n], b_send.at[h, n], b_recv.at[h, n], coredev).wait_recv()
            acc = acc + br[h, n].astype(jnp.float32)
        ms[h] = acc.astype(jnp.bfloat16)
        start(remote(ms.at[h], cb.at[h, 2 * u_own + k], m_send.at[h], m_recv.at[h], move_to(h)))

    def c_start(h):
        here = cb.at[h, cslot(h, False, 0)]
        remote(here, here, m_send.at[h], m_recv.at[h], move_to(h)).wait_recv()
        ag_start(C, h)

    def mm2(h, d):
        ag_x(C, h, d)
        for dz in around(d):
            u = turn(h, (z + dz - z_src) % 8)
            lhs = jnp.concatenate([cb[h, 2 * u], cb[h, 2 * u + 1]], axis=1)
            v = lax.dot_general(lhs, db[u], NT, preferred_element_type=jnp.float32)
            if d == 0:
                s[h] = v
            else:
                s[h] += v

    def half(q):
        return pl.ds(pl.multiple_of(q * 128, 128), 128)

    def e_copy(h):
        return remote(s.at[h, half(other)], dx.at[h], e_send.at[h], e_recv.at[h], coredev)

    def d_copy(h, n):
        jj = (j + n) % 8
        rows = pl.ds(pl.multiple_of(jj * 16, 16), 16)
        return remote(ds_.at[h, rows], dr.at[h, n], d_send.at[h, n], d_recv.at[h, n], plane(jj))

    def d_out(h):
        e_copy(h).wait_recv()
        ds_[h] = s[h, half(k)] + dx[h]
        for n in range(1, 8):
            start(d_copy(h, n))

    def d_red(h):
        acc = ds_[h, pl.ds(pl.multiple_of(j * 16, 16), 16)]
        for n in range(1, 8):
            d_copy(h, n).wait_recv()
            acc = acc + dr[h, n]
        out_ref[pl.ds(16 * h, 16)] = acc

    ag_start(A, 0)
    for c in sent[2:4]:
        c.wait_send()
    del sent[2:4]
    ag_start(A, 1)
    g_start()
    step(A, 0, 1)
    step(A, 1, 1)
    forward(0, 0)
    step(A, 0, 2)
    forward(1, 0)
    step(A, 1, 2)
    forward(0, 1)
    step(A, 0, 3)
    forward(1, 1)
    step(A, 1, 3)
    forward(0, 2)
    step(A, 0, 4)
    forward(0, 3)
    forward(0, 4)
    step(A, 1, 4)
    forward(1, 2)
    g_wait()
    forwarded(0)
    mm(0, 0)
    forward(1, 3)
    forward(1, 4)
    mm(0, 1)
    mm(0, 2)
    mm(0, 3)
    forwarded(1)
    for n in range(4):
        mm(1, n)
    for c in loads:
        if c[0] == "d":
            loads[c].wait()
    b_red(0)
    b_red(1)
    c_start(0)
    step(C, 0, 1)
    c_start(1)
    mm2(0, 0)
    step(C, 0, 2)
    step(C, 1, 1)
    mm2(0, 1)
    mm2(1, 0)
    step(C, 0, 3)
    step(C, 1, 2)
    mm2(0, 2)
    mm2(1, 1)
    step(C, 0, 4)
    mm2(0, 3)
    mm2(0, 4)
    start(e_copy(0))
    step(C, 1, 3)
    mm2(1, 2)
    d_out(0)
    step(C, 1, 4)
    mm2(1, 3)
    mm2(1, 4)
    start(e_copy(1))
    d_red(0)
    d_out(1)
    d_red(1)
    for c in sent:
        c.wait_send()
    for h in (0, 1):
        for n in range(1, 8):
            remote(bs.at[h, 0], br.at[h, n], b_send.at[h, n], b_recv.at[h, n], coredev).wait_send()


def body(test_block, inverse_gram, train_grads):
    bf, f32 = jnp.bfloat16, jnp.float32
    dma = pltpu.SemaphoreType.DMA
    return pl.pallas_call(
        kernel,
        out_shape=jax.ShapeDtypeStruct((32, 512), f32),
        in_specs=[pl.BlockSpec(memory_space=pl.ANY)] * 3,
        out_specs=pl.BlockSpec(memory_space=pltpu.VMEM),
        scratch_shapes=[
            pltpu.VMEM((2, 2, 2, 2, 4, 16, 2048), bf),
            pltpu.VMEM((2, 4, 2048, 256), bf),
            pltpu.VMEM((8, 512, 256), bf),
            pltpu.VMEM((2, 256, 128), f32),
            pltpu.VMEM((2, 8, 256, 128), bf),
            pltpu.VMEM((2, 8, 256, 128), bf),
            pltpu.VMEM((2, 256, 128), bf),
            pltpu.VMEM((2, 16, 256, 128), bf),
            pltpu.VMEM((2, 256, 512), f32),
            pltpu.VMEM((2, 128, 512), f32),
            pltpu.VMEM((2, 128, 512), f32),
            pltpu.VMEM((2, 8, 16, 512), f32),
            dma((22,)),
            dma((4, 33)), dma((4, 33)),
            dma((4,)), dma((4,)),
            dma((2, 8)), dma((2, 8)),
            dma((2, 8)), dma((2, 8)),
            dma((2,)), dma((2,)),
            dma((2,)), dma((2,)),
            dma((2, 8)), dma((2, 8)),
        ],
        compiler_params=pltpu.CompilerParams(
            collective_id=0, has_side_effects=True, vmem_limit_bytes=52 * 2**20
        ),
        cost_estimate=pl.CostEstimate(flops=5_400_000_000, bytes_accessed=11_000_000, transcendentals=0),
        name="scores_kernel",
    )(test_block, inverse_gram, train_grads)


def solution(mesh):
    return jax.shard_map(
        body,
        mesh=mesh,
        in_specs=(P("col", "row"), P("row", "col"), P("col", "row")),
        out_specs=P("row", "col"),
        check_vma=False,
    )
```

```python
import jax
import jax.numpy as jnp
from jax import lax
from jax.experimental import pallas as pl
from jax.experimental.pallas import tpu as pltpu
from jax.sharding import PartitionSpec as P

MESH = pl.DeviceIdType.MESH
A, C = 0, 1
CUT_A, CUT_C = 1024, 128
NT = (((1,), (1,)), ((), ()))


def kernel(
    t_hbm, g_hbm, d_hbm, out_ref,
    tb, gb, db, acc_, own, bs, br, ms, cb, s, dx, ds_, dr,
    load_sem, ag_send, ag_recv, g_send, g_recv, f_send, f_recv, b_send, b_recv,
    m_send, m_recv, e_send, e_recv, d_send, d_recv,
):
    row, col = lax.axis_index("row"), lax.axis_index("col")
    j, k = row // 2, row % 2
    xh, y = j // 4, j % 4
    xl, z = col // 8, col % 8
    other = 1 - k
    sigma = 2 * y + xh
    u_own = (sigma + 4 * k) % 8

    def chip(sg):
        return (sg % 2) * 4 + sg // 2

    def zdev(dz):
        return (row, xl * 8 + (z + dz) % 8)

    def xzdev(dz):
        return (row, (1 - xl) * 8 + (z + dz) % 8)

    xdev = xzdev(0)
    coredev = (j * 2 + other, col)

    def plane(jj):
        return (jj * 2 + k, col)

    def turn(h, u):
        return u if h == 0 else (8 - u) % 8

    def move_to(h):
        return (col, ((1 - k + z) % 2) * 8 + (z + turn(h, u_own)) % 8)

    z_src = 2 * y + k

    loads = {}

    def load(name, src, dst, sem):
        c = pltpu.make_async_copy(src, dst, load_sem.at[sem])
        c.start()
        loads[name] = c

    def tslot(h, c, mx, dz):
        zz, xx = (z + dz) % 8, jnp.where(mx, 1 - xl, xl)
        return tb.at[h, c, zz % 2, xx, zz // 2]

    def cslot(h, mx, dz):
        zz, xx = (z + dz) % 8, jnp.where(mx, 1 - xl, xl)
        return 2 * turn(h, (zz - z_src) % 8) + (1 + xx + k) % 2

    def tile(n):
        return (u_own // 2 + 1 + n) % 4

    for h in (0, 1):
        load(("t", h), t_hbm.at[pl.ds(16 * h, 16)], tslot(h, k, False, 0), h)
    for n in range(4):
        c0 = pl.multiple_of(k * 1024 + tile(n) * 256, 256)
        load(("g", n), g_hbm.at[:, pl.ds(c0, 256)], gb.at[k, tile(n)], 2 + n)
    for q in range(8):
        for kk in range(2):
            load(("d", q, kk), d_hbm.at[:, pl.ds(kk * 1024 + q * 128, 128)], db.at[q, :, pl.ds(kk * 128, 128)], 6 + 2 * q + kk)

    barrier = pltpu.get_barrier_semaphore()
    greet = [zdev(1), zdev(-1), xzdev(1), xzdev(-1), xdev, coredev]
    for to in greet + [plane((j + i) % 8) for i in range(1, 8)]:
        pl.semaphore_signal(barrier, inc=1, device_id=to, device_id_type=MESH)
    pl.semaphore_wait(barrier, 13)

    sent = []

    def remote(src, dst, ssem, rsem, to):
        return pltpu.make_async_remote_copy(
            src_ref=src, dst_ref=dst, send_sem=ssem, recv_sem=rsem, device_id=to, device_id_type=MESH
        )

    def start(c):
        c.start()
        sent.append(c)

    def block(ph, h, mx, dz, piece, origin=False):
        if ph == A:
            cut = pl.ds(0, CUT_A) if piece == "x" else pl.ds(CUT_A, 2048 - CUT_A)
            if origin and not mx and dz == 0:
                return t_hbm.at[pl.ds(16 * h, 16), cut]
            return tslot(h, k, mx, dz).at[:, cut]
        cut = pl.ds(0, CUT_C) if piece == "x" else pl.ds(CUT_C, 256 - CUT_C)
        return cb.at[h, cslot(h, mx, dz), cut]

    def message(ph, h, kind, way, d):
        i = 2 * ph + h
        if kind in "XY":
            piece, n = ("z", 24 + d % 8) if kind == "X" else ("x", 32)
            return (ph, h, False, d, piece), (ph, h, True, d, piece), i, n, xdev
        sign = 1 if way == 0 else -1
        if kind == "E":
            return (ph, h, False, -sign * 3, "z"), (ph, h, True, -sign * 4, "z"), i, 28, xzdev(sign)
        mx, piece = kind == "p", "z" if kind == "z" else "x"
        n = "zxp".index(kind) * 8 + way * 4 + d - 1
        if kind == "p" and d == 1:
            return (ph, h, False, 0, piece), (ph, h, True, -sign, piece), i, n, xzdev(sign)
        return (ph, h, mx, -sign * (d - 1), piece), (ph, h, mx, -sign * d, piece), i, n, zdev(sign)

    def send(ph, h, kind, way, d):
        src, _, i, n, to = message(ph, h, kind, way, d)
        start(remote(block(*src, origin=True), block(*src), ag_send.at[i, n], ag_recv.at[i, n], to))

    def arrived(ph, h, kind, way, d):
        _, dst, i, n, to = message(ph, h, kind, way, d)
        ref = block(*dst)
        remote(ref, ref, ag_send.at[i, n], ag_recv.at[i, n], to).wait_recv()

    def exists(h, kind, way, d):
        return d <= 3 or (d == 4 and (way == h) == (kind != "p"))

    def ag_start(ph, h):
        for kind in "pzx":
            for way in (0, 1):
                send(ph, h, kind, way, 1)
        send(ph, h, "Y", 0, 0)
        send(ph, h, "X", 0, 0)

    def ag(ph, h, kind, d):
        for way in (0, 1):
            if exists(h, kind, way, d):
                arrived(ph, h, kind, way, d)
                if exists(h, kind, way, d + 1):
                    send(ph, h, kind, way, d + 1)
                if kind == "z" and d == 3 and way == h:
                    send(ph, h, "E", way, 4)
                if kind == "z" and d < 4:
                    send(ph, h, "X", 0, -d if way == 0 else d)

    def step(ph, h, d):
        for kind in "zpx":
            ag(ph, h, kind, d)

    def around(d):
        return (0,) if d == 0 else (-d, d) if d < 4 else (4,)

    def ag_x(ph, h, d):
        for dz in around(d):
            arrived(ph, h, "X", 0, dz)
        if d == 0:
            arrived(ph, h, "Y", 0, 0)

    def f_copy(h, dz):
        zz = (z + dz) % 8
        ref = tb.at[h, k, zz % 2, :, zz // 2]
        return remote(ref, ref, f_send.at[h, dz % 8], f_recv.at[h, dz % 8], coredev)

    def forward(h, d):
        ag_x(A, h, d)
        if d == 0:
            loads[("t", h)].wait()
        for dz in around(d):
            start(f_copy(h, dz))

    def forwarded(h):
        for dz in range(8):
            zz = (z + dz) % 8
            ref = tb.at[h, other, zz % 2, :, zz // 2]
            remote(ref, ref, f_send.at[h, dz], f_recv.at[h, dz], coredev).wait_recv()

    def g_copy(n):
        c0 = pl.multiple_of(other * 1024 + n * 256, 256)
        return remote(g_hbm.at[:, pl.ds(c0, 256)], gb.at[k, n], g_send.at[n], g_recv.at[n], coredev)

    def g_start():
        for n in range(4):
            start(g_copy(n))

    def g_wait():
        for n in range(4):
            remote(gb.at[other, n], gb.at[other, n], g_send.at[n], g_recv.at[n], coredev).wait_recv()

    def mma(h, n):
        acc_[n] = jnp.dot(tb[h, k].reshape(256, 2048), gb[k, tile(n)], preferred_element_type=jnp.float32)

    def mm(h, n):
        nn = tile(n)
        p = jnp.dot(tb[h, other].reshape(256, 2048), gb[other, nn], preferred_element_type=jnp.float32)
        p = p + acc_[n]
        for e in (0, 1):
            u = 2 * nn + e
            pe = p[:, e * 128 : e * 128 + 128]

            def away():
                bs[h, u] = pe.astype(jnp.bfloat16)
                b_copy(h, u).start()

            if n < 3:
                away()
            else:
                pl.when(u != u_own)(away)

                @pl.when(u == u_own)
                def _():
                    own[h] = pe

    def b_copy(h, u):
        sg = (u - 4 * k) % 8
        n = (sg - sigma) % 8
        return remote(bs.at[h, u], br.at[h, n], b_send.at[h, n], b_recv.at[h, n], plane(chip(sg)))

    def b_red(h):
        acc = own[h]
        for n in range(1, 8):
            remote(bs.at[h, 0], br.at[h, n], b_send.at[h, n], b_recv.at[h, n], coredev).wait_recv()
            acc = acc + br[h, n].astype(jnp.float32)
        ms[h] = acc.astype(jnp.bfloat16)
        start(remote(ms.at[h], cb.at[h, 2 * u_own + k], m_send.at[h], m_recv.at[h], move_to(h)))

    def c_start(h):
        here = cb.at[h, cslot(h, False, 0)]
        remote(here, here, m_send.at[h], m_recv.at[h], move_to(h)).wait_recv()
        ag_start(C, h)

    def mm2(h, d):
        ag_x(C, h, d)
        for dz in around(d):
            u = turn(h, (z + dz - z_src) % 8)
            lhs = jnp.concatenate([cb[h, 2 * u], cb[h, 2 * u + 1]], axis=1)
            v = lax.dot_general(lhs, db[u], NT, preferred_element_type=jnp.float32)
            if d == 0:
                s[h] = v
            else:
                s[h] += v

    def half(q):
        return pl.ds(pl.multiple_of(q * 128, 128), 128)

    def e_copy(h):
        return remote(s.at[h, half(other)], dx.at[h], e_send.at[h], e_recv.at[h], coredev)

    def d_copy(h, n):
        jj = (j + n) % 8
        rows = pl.ds(pl.multiple_of(jj * 16, 16), 16)
        return remote(ds_.at[h, rows], dr.at[h, n], d_send.at[h, n], d_recv.at[h, n], plane(jj))

    def d_out(h):
        e_copy(h).wait_recv()
        ds_[h] = s[h, half(k)] + dx[h]
        for n in range(1, 8):
            start(d_copy(h, n))

    def d_red(h):
        acc = ds_[h, pl.ds(pl.multiple_of(j * 16, 16), 16)]
        for n in range(1, 8):
            d_copy(h, n).wait_recv()
            acc = acc + dr[h, n]
        out_ref[pl.ds(16 * h, 16)] = acc

    ag_start(A, 0)
    for c in sent[2:4]:
        c.wait_send()
    del sent[2:4]
    ag_start(A, 1)
    g_start()
    step(A, 0, 1)
    step(A, 1, 1)
    forward(0, 0)
    step(A, 0, 2)
    forward(1, 0)
    step(A, 1, 2)
    forward(0, 1)
    step(A, 0, 3)
    forward(1, 1)
    step(A, 1, 3)
    forward(0, 2)
    step(A, 0, 4)
    forward(0, 3)
    forward(0, 4)
    for n in range(4):
        loads[("g", n)].wait()
        mma(0, n)
    step(A, 1, 4)
    forward(1, 2)
    g_wait()
    forwarded(0)
    for n in range(4):
        mm(0, n)
    forward(1, 3)
    forward(1, 4)
    for n in range(4):
        mma(1, n)
    forwarded(1)
    for n in range(4):
        mm(1, n)
    for c in loads:
        if c[0] == "d":
            loads[c].wait()
    b_red(0)
    b_red(1)
    c_start(0)
    step(C, 0, 1)
    c_start(1)
    step(C, 0, 2)
    mm2(0, 0)
    step(C, 1, 1)
    mm2(0, 1)
    mm2(1, 0)
    step(C, 0, 3)
    step(C, 1, 2)
    mm2(0, 2)
    mm2(1, 1)
    step(C, 0, 4)
    mm2(0, 3)
    mm2(0, 4)
    start(e_copy(0))
    step(C, 1, 3)
    mm2(1, 2)
    d_out(0)
    step(C, 1, 4)
    mm2(1, 3)
    mm2(1, 4)
    start(e_copy(1))
    d_out(1)
    d_red(0)
    d_red(1)
    for c in sent:
        c.wait_send()
    for h in (0, 1):
        for n in range(1, 8):
            remote(bs.at[h, 0], br.at[h, n], b_send.at[h, n], b_recv.at[h, n], coredev).wait_send()


def body(test_block, inverse_gram, train_grads):
    bf, f32 = jnp.bfloat16, jnp.float32
    dma = pltpu.SemaphoreType.DMA
    return pl.pallas_call(
        kernel,
        out_shape=jax.ShapeDtypeStruct((32, 512), f32),
        in_specs=[pl.BlockSpec(memory_space=pl.ANY)] * 3,
        out_specs=pl.BlockSpec(memory_space=pltpu.VMEM),
        scratch_shapes=[
            pltpu.VMEM((2, 2, 2, 2, 4, 16, 2048), bf),
            pltpu.VMEM((2, 4, 2048, 256), bf),
            pltpu.VMEM((8, 512, 256), bf),
            pltpu.VMEM((4, 256, 256), f32),
            pltpu.VMEM((2, 256, 128), f32),
            pltpu.VMEM((2, 8, 256, 128), bf),
            pltpu.VMEM((2, 8, 256, 128), bf),
            pltpu.VMEM((2, 256, 128), bf),
            pltpu.VMEM((2, 16, 256, 128), bf),
            pltpu.VMEM((2, 256, 512), f32),
            pltpu.VMEM((2, 128, 512), f32),
            pltpu.VMEM((2, 128, 512), f32),
            pltpu.VMEM((2, 8, 16, 512), f32),
            dma((22,)),
            dma((4, 33)), dma((4, 33)),
            dma((4,)), dma((4,)),
            dma((2, 8)), dma((2, 8)),
            dma((2, 8)), dma((2, 8)),
            dma((2,)), dma((2,)),
            dma((2,)), dma((2,)),
            dma((2, 8)), dma((2, 8)),
        ],
        compiler_params=pltpu.CompilerParams(
            collective_id=0, has_side_effects=True, vmem_limit_bytes=52 * 2**20
        ),
        cost_estimate=pl.CostEstimate(flops=5_400_000_000, bytes_accessed=11_000_000, transcendentals=0),
        name="scores_kernel",
    )(test_block, inverse_gram, train_grads)


def solution(mesh):
    return jax.shard_map(
        body,
        mesh=mesh,
        in_specs=(P("col", "row"), P("row", "col"), P("col", "row")),
        out_specs=P("row", "col"),
        check_vma=False,
    )
```

```python
import jax
import jax.numpy as jnp
from jax import lax
from jax.experimental import pallas as pl
from jax.experimental.pallas import tpu as pltpu
from jax.sharding import PartitionSpec as P

MESH = pl.DeviceIdType.MESH
A, C = 0, 1
CUT_A, CUT_C = 1024, 128
NT = (((1,), (1,)), ((), ()))


def kernel(
    t_hbm, g_hbm, d_hbm, out_ref,
    tb, gb, db, acc_, own, bs, br, ms, cb, s, dx, ds_, dr,
    load_sem, ag_send, ag_recv, g_send, g_recv, f_send, f_recv, b_send, b_recv,
    m_send, m_recv, e_send, e_recv, d_send, d_recv,
):
    row, col = lax.axis_index("row"), lax.axis_index("col")
    j, k = row // 2, row % 2
    xh, y = j // 4, j % 4
    xl, z = col // 8, col % 8
    other = 1 - k
    sigma = 2 * y + xh
    u_own = (sigma + 4 * k) % 8

    def chip(sg):
        return (sg % 2) * 4 + sg // 2

    def zdev(dz):
        return (row, xl * 8 + (z + dz) % 8)

    def xzdev(dz):
        return (row, (1 - xl) * 8 + (z + dz) % 8)

    xdev = xzdev(0)
    coredev = (j * 2 + other, col)

    def plane(jj):
        return (jj * 2 + k, col)

    def turn(h, u):
        return u if h == 0 else (8 - u) % 8

    def move_to(h):
        return (col, ((1 - k + z) % 2) * 8 + (z + turn(h, u_own)) % 8)

    z_src = 2 * y + k

    barrier = pltpu.get_barrier_semaphore()
    greet = [zdev(1), zdev(-1), xzdev(1), xzdev(-1), xdev, coredev]
    for to in greet + [plane((j + i) % 8) for i in range(1, 8)]:
        pl.semaphore_signal(barrier, inc=1, device_id=to, device_id_type=MESH)

    loads = {}

    def load(name, src, dst, sem):
        c = pltpu.make_async_copy(src, dst, load_sem.at[sem])
        c.start()
        loads[name] = c

    def tslot(h, c, mx, dz):
        zz, xx = (z + dz) % 8, jnp.where(mx, 1 - xl, xl)
        return tb.at[h, c, zz % 2, xx, zz // 2]

    def cslot(h, mx, dz):
        zz, xx = (z + dz) % 8, jnp.where(mx, 1 - xl, xl)
        return 2 * turn(h, (zz - z_src) % 8) + (1 + xx + k) % 2

    def tile(n):
        return (u_own // 2 + 1 + n) % 4

    for h in (0, 1):
        load(("t", h), t_hbm.at[pl.ds(16 * h, 16)], tslot(h, k, False, 0), h)
    for n in range(4):
        c0 = pl.multiple_of(k * 1024 + tile(n) * 256, 256)
        load(("g", n), g_hbm.at[:, pl.ds(c0, 256)], gb.at[k, tile(n)], 2 + n)
    for q in range(8):
        for kk in range(2):
            load(("d", q, kk), d_hbm.at[:, pl.ds(kk * 1024 + q * 128, 128)], db.at[q, :, pl.ds(kk * 128, 128)], 6 + 2 * q + kk)

    pl.semaphore_wait(barrier, 13)

    sent = []

    def drain(keep):
        n = max(len(sent) - keep, 0)
        for c in sent[:n]:
            c.wait_send()
        del sent[:n]

    def remote(src, dst, ssem, rsem, to):
        return pltpu.make_async_remote_copy(
            src_ref=src, dst_ref=dst, send_sem=ssem, recv_sem=rsem, device_id=to, device_id_type=MESH
        )

    def start(c):
        c.start()
        sent.append(c)

    def block(ph, h, mx, dz, piece, origin=False):
        if ph == A:
            cut = pl.ds(0, CUT_A) if piece == "x" else pl.ds(CUT_A, 2048 - CUT_A)
            if origin and not mx and dz == 0:
                return t_hbm.at[pl.ds(16 * h, 16), cut]
            return tslot(h, k, mx, dz).at[:, cut]
        cut = pl.ds(0, CUT_C) if piece == "x" else pl.ds(CUT_C, 256 - CUT_C)
        return cb.at[h, cslot(h, mx, dz), cut]

    def message(ph, h, kind, way, d):
        i = 2 * ph + h
        if kind in "XY":
            piece, n = ("z", 24 + d % 8) if kind == "X" else ("x", 32)
            return (ph, h, False, d, piece), (ph, h, True, d, piece), i, n, xdev
        sign = 1 if way == 0 else -1
        if kind == "E":
            return (ph, h, False, -sign * 3, "z"), (ph, h, True, -sign * 4, "z"), i, 28, xzdev(sign)
        mx, piece = kind == "p", "z" if kind == "z" else "x"
        n = "zxp".index(kind) * 8 + way * 4 + d - 1
        if kind == "p" and d == 1:
            return (ph, h, False, 0, piece), (ph, h, True, -sign, piece), i, n, xzdev(sign)
        return (ph, h, mx, -sign * (d - 1), piece), (ph, h, mx, -sign * d, piece), i, n, zdev(sign)

    def send(ph, h, kind, way, d):
        src, _, i, n, to = message(ph, h, kind, way, d)
        start(remote(block(*src, origin=True), block(*src), ag_send.at[i, n], ag_recv.at[i, n], to))

    def arrived(ph, h, kind, way, d):
        _, dst, i, n, to = message(ph, h, kind, way, d)
        ref = block(*dst)
        remote(ref, ref, ag_send.at[i, n], ag_recv.at[i, n], to).wait_recv()

    def exists(h, kind, way, d):
        return d <= 3 or (d == 4 and (way == h) == (kind != "p"))

    def ag_start(ph, h):
        for kind in "pzx":
            for way in (0, 1):
                send(ph, h, kind, way, 1)
        send(ph, h, "Y", 0, 0)
        send(ph, h, "X", 0, 0)

    def ag(ph, h, kind, d):
        for way in (0, 1):
            if exists(h, kind, way, d):
                arrived(ph, h, kind, way, d)
                if exists(h, kind, way, d + 1):
                    send(ph, h, kind, way, d + 1)
                if kind == "z" and d == 3 and way == h:
                    send(ph, h, "E", way, 4)
                if kind == "z" and d < 4:
                    send(ph, h, "X", 0, -d if way == 0 else d)

    def step(ph, h, d):
        for kind in "zpx":
            ag(ph, h, kind, d)

    def around(d):
        return (0,) if d == 0 else (-d, d) if d < 4 else (4,)

    def ag_x(ph, h, d):
        for dz in around(d):
            arrived(ph, h, "X", 0, dz)
        if d == 0:
            arrived(ph, h, "Y", 0, 0)

    def f_copy(h, dz):
        zz = (z + dz) % 8
        ref = tb.at[h, k, zz % 2, :, zz // 2]
        return remote(ref, ref, f_send.at[h, dz % 8], f_recv.at[h, dz % 8], coredev)

    def forward(h, d):
        ag_x(A, h, d)
        if d == 0:
            loads[("t", h)].wait()
        for dz in around(d):
            start(f_copy(h, dz))

    def forwarded(h):
        for dz in range(8):
            zz = (z + dz) % 8
            ref = tb.at[h, other, zz % 2, :, zz // 2]
            remote(ref, ref, f_send.at[h, dz], f_recv.at[h, dz], coredev).wait_recv()

    def g_copy(n):
        c0 = pl.multiple_of(other * 1024 + n * 256, 256)
        return remote(g_hbm.at[:, pl.ds(c0, 256)], gb.at[k, n], g_send.at[n], g_recv.at[n], coredev)

    def g_start():
        for n in range(4):
            start(g_copy(n))

    def g_wait():
        for n in range(4):
            remote(gb.at[other, n], gb.at[other, n], g_send.at[n], g_recv.at[n], coredev).wait_recv()

    def mma(h, n):
        acc_[n] = jnp.dot(tb[h, k].reshape(256, 2048), gb[k, tile(n)], preferred_element_type=jnp.float32)

    def mm(h, n):
        nn = tile(n)
        p = jnp.dot(tb[h, other].reshape(256, 2048), gb[other, nn], preferred_element_type=jnp.float32)
        p = p + acc_[n]
        for e in (0, 1):
            u = 2 * nn + e
            pe = p[:, e * 128 : e * 128 + 128]

            def away():
                bs[h, u] = pe.astype(jnp.bfloat16)
                b_copy(h, u).start()

            if n < 3:
                away()
            else:
                pl.when(u != u_own)(away)

                @pl.when(u == u_own)
                def _():
                    own[h] = pe

    def b_copy(h, u):
        sg = (u - 4 * k) % 8
        n = (sg - sigma) % 8
        return remote(bs.at[h, u], br.at[h, n], b_send.at[h, n], b_recv.at[h, n], plane(chip(sg)))

    def b_left(h):
        for n in range(1, 8):
            remote(bs.at[h, 0], br.at[h, n], b_send.at[h, n], b_recv.at[h, n], coredev).wait_send()

    def b_red(h):
        acc = own[h]
        for n in range(1, 8):
            remote(bs.at[h, 0], br.at[h, n], b_send.at[h, n], b_recv.at[h, n], coredev).wait_recv()
            acc = acc + br[h, n].astype(jnp.float32)
        ms[h] = acc.astype(jnp.bfloat16)
        start(remote(ms.at[h], cb.at[h, 2 * u_own + k], m_send.at[h], m_recv.at[h], move_to(h)))

    def c_start(h):
        here = cb.at[h, cslot(h, False, 0)]
        remote(here, here, m_send.at[h], m_recv.at[h], move_to(h)).wait_recv()
        ag_start(C, h)

    def mm2(h, d):
        ag_x(C, h, d)
        for dz in around(d):
            u = turn(h, (z + dz - z_src) % 8)
            lhs = jnp.concatenate([cb[h, 2 * u], cb[h, 2 * u + 1]], axis=1)
            v = lax.dot_general(lhs, db[u], NT, preferred_element_type=jnp.float32)
            if d == 0:
                s[h] = v
            else:
                s[h] += v

    def half(q):
        return pl.ds(pl.multiple_of(q * 128, 128), 128)

    def e_copy(h):
        return remote(s.at[h, half(other)], dx.at[h], e_send.at[h], e_recv.at[h], coredev)

    def d_copy(h, n):
        jj = (j + n) % 8
        rows = pl.ds(pl.multiple_of(jj * 16, 16), 16)
        return remote(ds_.at[h, rows], dr.at[h, n], d_send.at[h, n], d_recv.at[h, n], plane(jj))

    def d_out(h):
        e_copy(h).wait_recv()
        ds_[h] = s[h, half(k)] + dx[h]
        for n in range(1, 8):
            start(d_copy(h, n))

    def d_red(h):
        acc = ds_[h, pl.ds(pl.multiple_of(j * 16, 16), 16)]
        for n in range(1, 8):
            d_copy(h, n).wait_recv()
            acc = acc + dr[h, n]
        out_ref[pl.ds(16 * h, 16)] = acc

    ag_start(A, 0)
    ag_start(A, 1)
    step(A, 0, 1)
    step(A, 1, 1)
    g_start()
    forward(0, 0)
    step(A, 0, 2)
    forward(1, 0)
    step(A, 1, 2)
    forward(0, 1)
    step(A, 0, 3)
    forward(1, 1)
    step(A, 1, 3)
    forward(0, 2)
    step(A, 0, 4)
    forward(0, 3)
    forward(0, 4)
    for n in range(4):
        loads[("g", n)].wait()
        mma(0, n)
    step(A, 1, 4)
    forward(1, 2)
    g_wait()
    forwarded(0)
    for n in range(4):
        mm(0, n)
    forward(1, 3)
    forward(1, 4)
    for n in range(4):
        mma(1, n)
    forwarded(1)
    for n in range(4):
        mm(1, n)
    for c in loads:
        if c[0] == "d":
            loads[c].wait()
    drain(0)
    b_red(0)
    b_red(1)
    c_start(0)
    step(C, 0, 1)
    c_start(1)
    step(C, 0, 2)
    mm2(0, 0)
    step(C, 1, 1)
    mm2(0, 1)
    mm2(1, 0)
    step(C, 0, 3)
    step(C, 1, 2)
    mm2(0, 2)
    mm2(1, 1)
    step(C, 0, 4)
    mm2(0, 3)
    mm2(0, 4)
    start(e_copy(0))
    step(C, 1, 3)
    mm2(1, 2)
    d_out(0)
    b_left(0)
    b_left(1)
    drain(40)
    step(C, 1, 4)
    mm2(1, 3)
    mm2(1, 4)
    start(e_copy(1))
    d_out(1)
    d_red(0)
    d_red(1)
    for c in sent:
        c.wait_send()


def body(test_block, inverse_gram, train_grads):
    bf, f32 = jnp.bfloat16, jnp.float32
    dma = pltpu.SemaphoreType.DMA
    return pl.pallas_call(
        kernel,
        out_shape=jax.ShapeDtypeStruct((32, 512), f32),
        in_specs=[pl.BlockSpec(memory_space=pl.ANY)] * 3,
        out_specs=pl.BlockSpec(memory_space=pltpu.VMEM),
        scratch_shapes=[
            pltpu.VMEM((2, 2, 2, 2, 4, 16, 2048), bf),
            pltpu.VMEM((2, 4, 2048, 256), bf),
            pltpu.VMEM((8, 512, 256), bf),
            pltpu.VMEM((4, 256, 256), f32),
            pltpu.VMEM((2, 256, 128), f32),
            pltpu.VMEM((2, 8, 256, 128), bf),
            pltpu.VMEM((2, 8, 256, 128), bf),
            pltpu.VMEM((2, 256, 128), bf),
            pltpu.VMEM((2, 16, 256, 128), bf),
            pltpu.VMEM((2, 256, 512), f32),
            pltpu.VMEM((2, 128, 512), f32),
            pltpu.VMEM((2, 128, 512), f32),
            pltpu.VMEM((2, 8, 16, 512), f32),
            dma((22,)),
            dma((4, 33)), dma((4, 33)),
            dma((4,)), dma((4,)),
            dma((2, 8)), dma((2, 8)),
            dma((2, 8)), dma((2, 8)),
            dma((2,)), dma((2,)),
            dma((2,)), dma((2,)),
            dma((2, 8)), dma((2, 8)),
        ],
        compiler_params=pltpu.CompilerParams(
            collective_id=0, has_side_effects=True, vmem_limit_bytes=52 * 2**20
        ),
        cost_estimate=pl.CostEstimate(flops=5_400_000_000, bytes_accessed=11_000_000, transcendentals=0),
        name="scores_kernel",
    )(test_block, inverse_gram, train_grads)


def solution(mesh):
    return jax.shard_map(
        body,
        mesh=mesh,
        in_specs=(P("col", "row"), P("row", "col"), P("col", "row")),
        out_specs=P("row", "col"),
        check_vma=False,
    )
```

```python
import jax
import jax.numpy as jnp
from jax import lax
from jax.experimental import pallas as pl
from jax.experimental.pallas import tpu as pltpu
from jax.sharding import PartitionSpec as P

MESH = pl.DeviceIdType.MESH
A, C = 0, 1
CUT_A, CUT_C = 1024, 128
NT = (((1,), (1,)), ((), ()))


def kernel(
    t_hbm, g_hbm, d_hbm, out_ref,
    tb, gb, db, acc_, own, bs, br, ms, cb, s, dx, ds_, dr,
    load_sem, ag_send, ag_recv, g_send, g_recv, f_send, f_recv, b_send, b_recv,
    m_send, m_recv, e_send, e_recv, d_send, d_recv,
):
    row, col = lax.axis_index("row"), lax.axis_index("col")
    j, k = row // 2, row % 2
    xh, y = j // 4, j % 4
    xl, z = col // 8, col % 8
    other = 1 - k
    sigma = 2 * y + xh
    u_own = (sigma + 4 * k) % 8

    def chip(sg):
        return (sg % 2) * 4 + sg // 2

    def zdev(dz):
        return (row, xl * 8 + (z + dz) % 8)

    def xzdev(dz):
        return (row, (1 - xl) * 8 + (z + dz) % 8)

    xdev = xzdev(0)
    coredev = (j * 2 + other, col)

    def plane(jj):
        return (jj * 2 + k, col)

    def turn(h, u):
        return u if h == 0 else (8 - u) % 8

    def move_to(h):
        return (col, ((1 - k + z) % 2) * 8 + (z + turn(h, u_own)) % 8)

    z_src = 2 * y + k

    barrier = pltpu.get_barrier_semaphore()
    greet = [zdev(1), zdev(-1), xzdev(1), xzdev(-1), xdev, coredev]
    for to in greet + [plane((j + i) % 8) for i in range(1, 8)]:
        pl.semaphore_signal(barrier, inc=1, device_id=to, device_id_type=MESH)

    loads = {}

    def load(name, src, dst, sem):
        c = pltpu.make_async_copy(src, dst, load_sem.at[sem])
        c.start()
        loads[name] = c

    def tslot(h, c, mx, dz):
        zz, xx = (z + dz) % 8, jnp.where(mx, 1 - xl, xl)
        return tb.at[h, c, zz % 2, xx, zz // 2]

    def cslot(h, mx, dz):
        zz, xx = (z + dz) % 8, jnp.where(mx, 1 - xl, xl)
        return 2 * turn(h, (zz - z_src) % 8) + (1 + xx + k) % 2

    def tile(n):
        return (u_own // 2 + 1 + n) % 4

    for h in (0, 1):
        load(("t", h), t_hbm.at[pl.ds(16 * h, 16)], tslot(h, k, False, 0), h)
    for n in range(4):
        c0 = pl.multiple_of(k * 1024 + tile(n) * 256, 256)
        load(("g", n), g_hbm.at[:, pl.ds(c0, 256)], gb.at[k, tile(n)], 2 + n)
    for q in range(8):
        for kk in range(2):
            load(("d", q, kk), d_hbm.at[:, pl.ds(kk * 1024 + q * 128, 128)], db.at[q, :, pl.ds(kk * 128, 128)], 6 + 2 * q + kk)

    pl.semaphore_wait(barrier, 13)

    sent = []

    def drain(keep):
        n = max(len(sent) - keep, 0)
        for c in sent[:n]:
            c.wait_send()
        del sent[:n]

    def remote(src, dst, ssem, rsem, to):
        return pltpu.make_async_remote_copy(
            src_ref=src, dst_ref=dst, send_sem=ssem, recv_sem=rsem, device_id=to, device_id_type=MESH
        )

    def start(c):
        c.start()
        sent.append(c)

    def block(ph, h, mx, dz, piece, origin=False):
        if piece == "w":
            if ph == C:
                return cb.at[h, cslot(h, mx, dz)]
            if origin and not mx and dz == 0:
                return t_hbm.at[pl.ds(16 * h, 16)]
            return tslot(h, k, mx, dz)
        if ph == A:
            cut = pl.ds(0, CUT_A) if piece == "x" else pl.ds(CUT_A, 2048 - CUT_A)
            if origin and not mx and dz == 0:
                return t_hbm.at[pl.ds(16 * h, 16), cut]
            return tslot(h, k, mx, dz).at[:, cut]
        cut = pl.ds(0, CUT_C) if piece == "x" else pl.ds(CUT_C, 256 - CUT_C)
        return cb.at[h, cslot(h, mx, dz), cut]

    def message(ph, h, kind, way, d):
        i = 2 * ph + h
        if kind in "XY":
            piece, n = ("z", 24 + d % 8) if kind == "X" else ("x", 32)
            return (ph, h, False, d, piece), (ph, h, True, d, piece), i, n, xdev
        sign = 1 if way == 0 else -1
        if kind == "E":
            return (ph, h, False, -sign * 3, "z"), (ph, h, True, -sign * 4, "z"), i, 28, xzdev(sign)
        mx, piece = kind == "p", "w" if kind == "w" else "x"
        n = "wxp".index(kind) * 8 + way * 4 + d - 1
        if kind == "p" and d == 1:
            return (ph, h, False, 0, piece), (ph, h, True, -sign, piece), i, n, xzdev(sign)
        return (ph, h, mx, -sign * (d - 1), piece), (ph, h, mx, -sign * d, piece), i, n, zdev(sign)

    def send(ph, h, kind, way, d):
        src, _, i, n, to = message(ph, h, kind, way, d)
        start(remote(block(*src, origin=True), block(*src), ag_send.at[i, n], ag_recv.at[i, n], to))

    def arrived(ph, h, kind, way, d):
        _, dst, i, n, to = message(ph, h, kind, way, d)
        ref = block(*dst)
        remote(ref, ref, ag_send.at[i, n], ag_recv.at[i, n], to).wait_recv()

    def exists(h, kind, way, d):
        return d <= 3 or (d == 4 and (way == h) == (kind != "p"))

    def ag_start(ph, h):
        for kind in "pw":
            for way in (0, 1):
                send(ph, h, kind, way, 1)
        send(ph, h, "Y", 0, 0)
        send(ph, h, "X", 0, 0)

    def ag(ph, h, kind, d):
        for way in (0, 1):
            if exists(h, kind, way, d):
                arrived(ph, h, kind, way, d)
                if exists(h, kind, way, d + 1):
                    send(ph, h, kind, way, d + 1)
                if kind == "w" and d == 3 and way == h:
                    send(ph, h, "E", way, 4)
                if kind == "w" and d < 4:
                    send(ph, h, "X", 0, -d if way == 0 else d)

    def step(ph, h, d):
        for kind in "wp":
            ag(ph, h, kind, d)

    def around(d):
        return (0,) if d == 0 else (-d, d) if d < 4 else (4,)

    def ag_x(ph, h, d):
        for dz in around(d):
            arrived(ph, h, "X", 0, dz)
        if d == 0:
            arrived(ph, h, "Y", 0, 0)

    def f_copy(h, dz):
        zz = (z + dz) % 8
        ref = tb.at[h, k, zz % 2, :, zz // 2]
        return remote(ref, ref, f_send.at[h, dz % 8], f_recv.at[h, dz % 8], coredev)

    def forward(h, d):
        ag_x(A, h, d)
        if d == 0:
            loads[("t", h)].wait()
        for dz in around(d):
            start(f_copy(h, dz))

    def forwarded(h):
        for dz in range(8):
            zz = (z + dz) % 8
            ref = tb.at[h, other, zz % 2, :, zz // 2]
            remote(ref, ref, f_send.at[h, dz], f_recv.at[h, dz], coredev).wait_recv()

    def g_copy(n):
        c0 = pl.multiple_of(other * 1024 + n * 256, 256)
        return remote(g_hbm.at[:, pl.ds(c0, 256)], gb.at[k, n], g_send.at[n], g_recv.at[n], coredev)

    def g_start():
        for n in range(4):
            start(g_copy(n))

    def g_wait():
        for n in range(4):
            remote(gb.at[other, n], gb.at[other, n], g_send.at[n], g_recv.at[n], coredev).wait_recv()

    def mma(h, n):
        acc_[n] = jnp.dot(tb[h, k].reshape(256, 2048), gb[k, tile(n)], preferred_element_type=jnp.float32)

    def mm(h, n):
        nn = tile(n)
        p = jnp.dot(tb[h, other].reshape(256, 2048), gb[other, nn], preferred_element_type=jnp.float32)
        p = p + acc_[n]
        for e in (0, 1):
            u = 2 * nn + e
            pe = p[:, e * 128 : e * 128 + 128]

            def away():
                bs[h, u] = pe.astype(jnp.bfloat16)
                b_copy(h, u).start()

            if n < 3:
                away()
            else:
                pl.when(u != u_own)(away)

                @pl.when(u == u_own)
                def _():
                    own[h] = pe

    def b_copy(h, u):
        sg = (u - 4 * k) % 8
        n = (sg - sigma) % 8
        return remote(bs.at[h, u], br.at[h, n], b_send.at[h, n], b_recv.at[h, n], plane(chip(sg)))

    def b_left(h):
        for n in range(1, 8):
            remote(bs.at[h, 0], br.at[h, n], b_send.at[h, n], b_recv.at[h, n], coredev).wait_send()

    def b_red(h):
        acc = own[h]
        for n in range(1, 8):
            remote(bs.at[h, 0], br.at[h, n], b_send.at[h, n], b_recv.at[h, n], coredev).wait_recv()
            acc = acc + br[h, n].astype(jnp.float32)
        ms[h] = acc.astype(jnp.bfloat16)
        start(remote(ms.at[h], cb.at[h, 2 * u_own + k], m_send.at[h], m_recv.at[h], move_to(h)))

    def c_start(h):
        here = cb.at[h, cslot(h, False, 0)]
        remote(here, here, m_send.at[h], m_recv.at[h], move_to(h)).wait_recv()
        ag_start(C, h)

    def mm2(h, d):
        ag_x(C, h, d)
        for dz in around(d):
            u = turn(h, (z + dz - z_src) % 8)
            lhs = jnp.concatenate([cb[h, 2 * u], cb[h, 2 * u + 1]], axis=1)
            v = lax.dot_general(lhs, db[u], NT, preferred_element_type=jnp.float32)
            if d == 0:
                s[h] = v
            else:
                s[h] += v

    def half(q):
        return pl.ds(pl.multiple_of(q * 128, 128), 128)

    def e_copy(h):
        return remote(s.at[h, half(other)], dx.at[h], e_send.at[h], e_recv.at[h], coredev)

    def d_copy(h, n):
        jj = (j + n) % 8
        rows = pl.ds(pl.multiple_of(jj * 16, 16), 16)
        return remote(ds_.at[h, rows], dr.at[h, n], d_send.at[h, n], d_recv.at[h, n], plane(jj))

    def d_out(h):
        e_copy(h).wait_recv()
        ds_[h] = s[h, half(k)] + dx[h]
        for n in range(1, 8):
            start(d_copy(h, n))

    def d_red(h):
        acc = ds_[h, pl.ds(pl.multiple_of(j * 16, 16), 16)]
        for n in range(1, 8):
            d_copy(h, n).wait_recv()
            acc = acc + dr[h, n]
        out_ref[pl.ds(16 * h, 16)] = acc

    ag_start(A, 0)
    ag_start(A, 1)
    step(A, 0, 1)
    step(A, 1, 1)
    g_start()
    forward(0, 0)
    step(A, 0, 2)
    forward(1, 0)
    step(A, 1, 2)
    forward(0, 1)
    step(A, 0, 3)
    forward(1, 1)
    step(A, 1, 3)
    forward(0, 2)
    step(A, 0, 4)
    forward(0, 3)
    forward(0, 4)
    for n in range(4):
        loads[("g", n)].wait()
        mma(0, n)
    step(A, 1, 4)
    forward(1, 2)
    g_wait()
    forwarded(0)
    for n in range(4):
        mm(0, n)
    forward(1, 3)
    forward(1, 4)
    for n in range(4):
        mma(1, n)
    forwarded(1)
    for n in range(4):
        mm(1, n)
    for c in loads:
        if c[0] == "d":
            loads[c].wait()
    drain(0)
    b_red(0)
    b_red(1)
    c_start(0)
    step(C, 0, 1)
    c_start(1)
    step(C, 0, 2)
    mm2(0, 0)
    step(C, 1, 1)
    mm2(0, 1)
    mm2(1, 0)
    step(C, 0, 3)
    step(C, 1, 2)
    mm2(0, 2)
    mm2(1, 1)
    step(C, 0, 4)
    mm2(0, 3)
    mm2(0, 4)
    start(e_copy(0))
    step(C, 1, 3)
    mm2(1, 2)
    d_out(0)
    b_left(0)
    b_left(1)
    drain(40)
    step(C, 1, 4)
    mm2(1, 3)
    mm2(1, 4)
    start(e_copy(1))
    d_out(1)
    d_red(0)
    d_red(1)
    for c in sent:
        c.wait_send()


def body(test_block, inverse_gram, train_grads):
    bf, f32 = jnp.bfloat16, jnp.float32
    dma = pltpu.SemaphoreType.DMA
    return pl.pallas_call(
        kernel,
        out_shape=jax.ShapeDtypeStruct((32, 512), f32),
        in_specs=[pl.BlockSpec(memory_space=pl.ANY)] * 3,
        out_specs=pl.BlockSpec(memory_space=pltpu.VMEM),
        scratch_shapes=[
            pltpu.VMEM((2, 2, 2, 2, 4, 16, 2048), bf),
            pltpu.VMEM((2, 4, 2048, 256), bf),
            pltpu.VMEM((8, 512, 256), bf),
            pltpu.VMEM((4, 256, 256), f32),
            pltpu.VMEM((2, 256, 128), f32),
            pltpu.VMEM((2, 8, 256, 128), bf),
            pltpu.VMEM((2, 8, 256, 128), bf),
            pltpu.VMEM((2, 256, 128), bf),
            pltpu.VMEM((2, 16, 256, 128), bf),
            pltpu.VMEM((2, 256, 512), f32),
            pltpu.VMEM((2, 128, 512), f32),
            pltpu.VMEM((2, 128, 512), f32),
            pltpu.VMEM((2, 8, 16, 512), f32),
            dma((22,)),
            dma((4, 33)), dma((4, 33)),
            dma((4,)), dma((4,)),
            dma((2, 8)), dma((2, 8)),
            dma((2, 8)), dma((2, 8)),
            dma((2,)), dma((2,)),
            dma((2,)), dma((2,)),
            dma((2, 8)), dma((2, 8)),
        ],
        compiler_params=pltpu.CompilerParams(
            collective_id=0, has_side_effects=True, vmem_limit_bytes=52 * 2**20
        ),
        cost_estimate=pl.CostEstimate(flops=5_400_000_000, bytes_accessed=11_000_000, transcendentals=0),
        name="scores_kernel",
    )(test_block, inverse_gram, train_grads)


def solution(mesh):
    return jax.shard_map(
        body,
        mesh=mesh,
        in_specs=(P("col", "row"), P("row", "col"), P("col", "row")),
        out_specs=P("row", "col"),
        check_vma=False,
    )
```
